32 devices in a mesh: groups: 2 (over y), dp: 4 (over x, core), expert: 4 (over z).
Axes of the slice: x: 2, y: 2, z: 4, core: 2. Of those that a mesh axis runs over, the one named last changes fastest.
Arguments:
- tokens: bfloat16 [1024, 3072], P(('groups', 'dp'), 'expert'), parts along dimension 0, may hold values from -6 to 6
- cotangent: bfloat16 [1024, 3072], P(('groups', 'dp'), 'expert'), parts along dimension 0, may hold values from -6 to 6
- routes: int32 [1024, 2], P(('groups', 'dp')), parts along dimension 0, may hold values from 0 to 3, all different within a row; in each aligned block of 128 rows (0 to 127, 128 to 255, ...) at most 64 rows name the same one
- route_weight: float32 [1024, 2], P(('groups', 'dp')), parts along dimension 0, may hold values from 0.2 to 1
- tenant: int32 [1024], P(('groups', 'dp')), parts along dimension 0, may hold values from 0 to 1
- w_gate: bfloat16 [4, 3072, 8192], P('dp', None, 'expert'), may hold values from -0.109375 to 0.109375
- w_up: bfloat16 [4, 3072, 8192], P('dp', None, 'expert'), may hold values from -0.109375 to 0.109375
- w_down: bfloat16 [4, 8192, 3072], P('dp', 'expert'), may hold values from -0.0625 to 0.0625
- a_up: bfloat16 [4, 3072, 64], P('dp', 'expert'), may hold values from -0.109375 to 0.109375
- b_up: bfloat16 [4, 64, 8192], P('dp', None, 'expert'), may hold values from -1 to 1
- a_down: bfloat16 [4, 8192, 64], P('dp', 'expert'), may hold values from -0.0625 to 0.0625
- b_down: bfloat16 [4, 64, 3072], P('dp', None, 'expert'), may hold values from -1 to 1
Outputs:
- mixed: bfloat16 [1024, 3072], P(('groups', 'dp'), 'expert'), parts along dimension 0
- grad_a_up: float32 [8, 3072, 64], P(('groups', 'dp'), 'expert'), parts along dimension 0
- grad_b_up: float32 [8, 64, 8192], P(('groups', 'dp'), None, 'expert'), parts along dimension 0
- grad_a_down: float32 [8, 8192, 64], P(('groups', 'dp'), 'expert'), parts along dimension 0
- grad_b_down: float32 [8, 64, 3072], P(('groups', 'dp'), None, 'expert'), parts along dimension 0
The draws below stay inside these ranges and needn't reach their ends.
There are 2 independent parts, one for each index of `groups`. The reference program is written for one: setup_inputs(seed, part) draws one part's arguments, and reference() takes and returns one part's arrays. A program takes and returns all parts, laid end to end along the dimension named above; an argument that names none is the same for every part. Nothing has to cross between parts.
Inputs may be any that keep to these rules, and one draw needn't show every extreme that they name: `routes`: each token names 2 different experts. Within the 128 tokens of one index of dp (aligned blocks of rows) no expert is named more than 64 times, and in some block some expert is named exactly 64 times.
All inputs are finite; a program needn't handle non-finite values.
Results may differ from the reference program's by a relative error of at most 0.006.
Values may be sent and summed in bfloat16 or wider, within the bound.
A program may use at most 128 MiB of HBM per device.

```python
import math
import jax
import jax.numpy as jnp
import numpy as np
from jax import lax

D = 3072
FF = 8192
EXPERTS = 4
TOP = 2
RANK = 32
TENANTS = 2
TOK_DEV = 128
CAP = 64
TOKENS = 512
N_DP = 4


def set_ends(values, own_key, least, top_value):
    index_at = [jax.random.randint(jax.random.fold_in(own_key, axis), (), 0, length) for axis, length in enumerate(values.shape)]
    main_axis = values.shape.index(max(values.shape))
    beside = index_at[:main_axis] + [(index_at[main_axis] + 1) % values.shape[main_axis]] + index_at[main_axis + 1:]
    return values.at[tuple(index_at)].set(least).at[tuple(beside)].set(top_value)


def block_levels(key, shape, shards, low, top_value):
    def one(dim, parts):
        heights = jax.random.uniform(jax.random.fold_in(jax.random.fold_in(key, 6), dim), (parts,), jnp.float32, low / len(shards), top_value / len(shards))
        return jnp.repeat(jnp.exp(heights), shape[dim] // parts).reshape((-1,) + (1,) * (len(shape) - dim - 1))

    level = one(*shards[0])
    for cut in shards[1:]:
        level = level * one(*cut)
    return level


def deal_out(own_key, own, number, rows, amount, top, limit, lean):
    sequence = jax.random.permutation(own_key, amount)
    packed, usual = shares(amount, rows * top, limit, lean, True), shares(amount, rows * top, limit, lean, False)
    places = jnp.arange(amount)

    def named(sizes, offset_by):
        used = int((sizes > 0).sum())
        fixed = max(1, used // 4)
        passed = fixed + (places - fixed + offset_by * (used - fixed)) % max(1, amount - fixed)
        return jnp.zeros((amount,), jnp.int32).at[sequence[jnp.where(places < fixed, places, passed)]].set(jnp.asarray(sizes, jnp.int32))

    sizes = jnp.where(number % 4 == 0, named(packed, number // 4), named(usual, number - number // 4 - 1))
    mixed = jax.random.permutation(jax.random.fold_in(own, 3), amount)
    source_of, receiver = mixed[0:amount // 2 * 2:2], mixed[1:amount // 2 * 2:2]
    room = jnp.minimum(sizes[source_of] - 1, limit - sizes[receiver]) // 2
    room = jnp.where((source_of == sequence[0]) | (receiver == sequence[0]) | (sizes[receiver] == 0), 0, jnp.maximum(room, 0))
    passed = jax.random.randint(jax.random.fold_in(own, 4), (amount // 2,), 0, 1 << 20) % (room + 1)
    sizes = sizes.at[source_of].add(-passed).at[receiver].add(passed)
    members = jnp.searchsorted(jnp.cumsum(sizes), jnp.arange(rows * top), side="right").astype(jnp.int32)
    table = members.reshape(top, rows).T
    table = table[jax.random.permutation(jax.random.fold_in(own, 1), rows)]
    offset_by = jax.random.randint(jax.random.fold_in(own, 2), (rows, 1), 0, top)
    return jnp.take_along_axis(table, (jnp.arange(top)[None, :] + offset_by) % top, axis=1)


def shares(number_of, total, most, lean, full):
    weights = [(1 << 20) // math.isqrt(grade ** lean) + 1 for grade in range(1, number_of + 1)]
    largest = most if full else min(most, max(-(-total // number_of), total * weights[0] // sum(weights)))
    least = 1 if total - largest >= number_of - 1 else 0
    counts, rest = [largest] + [least] * (number_of - 1), total - largest - least * (number_of - 1)
    while rest > 0:
        candidates = [i for i in range(1, number_of) if counts[i] < largest] or [i for i in range(1, number_of) if counts[i] < most]
        pool, remaining = sum([weights[i] for i in candidates]), rest
        for i in candidates:
            addition = min(most - counts[i], max(1, remaining * weights[i] // pool), rest)
            counts[i] = counts[i] + addition
            rest = rest - addition
    return np.array(counts)


def centred(key, extent, deviation, most, pieces=(), kind=jnp.bfloat16):
    array = deviation * jax.random.normal(key, extent, jnp.float32)
    if pieces:
        array = array * block_levels(key, extent, pieces, -0.22, 0.18)
    return jnp.clip(array, -most, most).astype(kind)


def setup_inputs(seed: int = 0, part: int = 0) -> dict:
    seeds = jax.random.split(jax.random.key(seed), 13)
    part_splits = jax.random.split(jax.random.fold_in(seeds[12], part), 13)
    tokens = centred(part_splits[0], (TOKENS, D), 1.0, 6.0, ((0, 4), (1, 4)))
    cotangent = centred(part_splits[1], (TOKENS, D), 1.0, 6.0, ((0, 4), (1, 4)))
    routes_keys = jax.random.split(jax.random.fold_in(part_splits[2], 1), TOKENS // TOK_DEV)
    routes_turns = jax.random.permutation(jax.random.fold_in(part_splits[2], 3), TOKENS // TOK_DEV)
    routes = jax.vmap(lambda own, number: deal_out(jax.random.fold_in(part_splits[2], 2), own, number, TOK_DEV, EXPERTS, TOP, CAP, 2))(routes_keys, routes_turns).reshape((TOKENS, TOP))
    route_weight = jnp.clip(0.2 + 0.8 * jax.random.uniform(part_splits[3], (TOKENS, TOP), jnp.float32) ** block_levels(part_splits[3], (TOKENS, TOP), ((0, 4),), -0.2, 0.2), 0.2, 1.0)
    tenant = set_ends(jax.random.randint(part_splits[4], (TOKENS,), 0, TENANTS), jax.random.fold_in(part_splits[4], 1), 0, TENANTS - 1).astype(jnp.int32)
    w_gate = centred(seeds[5], (EXPERTS, D, FF), D ** -0.5, 0.109375, ((0, 4), (2, 4)))
    w_up = centred(seeds[6], (EXPERTS, D, FF), D ** -0.5, 0.109375, ((0, 4), (2, 4)))
    w_down = centred(seeds[7], (EXPERTS, FF, D), FF ** -0.5, 0.0625, ((0, 4), (1, 4)))
    a_up = centred(seeds[8], (EXPERTS, D, TENANTS * RANK), D ** -0.5, 0.109375, ((0, 4), (1, 4)))
    b_up = centred(seeds[9], (EXPERTS, TENANTS * RANK, FF), RANK ** -0.5, 1.0, ((0, 4), (2, 4)))
    a_down = centred(seeds[10], (EXPERTS, FF, TENANTS * RANK), FF ** -0.5, 0.0625, ((0, 4), (1, 4)))
    b_down = centred(seeds[11], (EXPERTS, TENANTS * RANK, D), RANK ** -0.5, 1.0, ((0, 4), (2, 4)))
    return dict(tokens=tokens, cotangent=cotangent, routes=routes, route_weight=route_weight, tenant=tenant, w_gate=w_gate, w_up=w_up, w_down=w_down, a_up=a_up, b_up=b_up, a_down=a_down, b_down=b_down)


adapter_scale = 0.5


def slot_table(route_rows, expert_count, slot_count):
    flat = route_rows.reshape(-1)
    order = jnp.arange(flat.shape[0], dtype=jnp.int32)
    earlier = (flat[:, None] == flat[None, :]) & (order[None, :] < order[:, None])
    rank = jnp.sum(earlier.astype(jnp.int32), axis=1)
    expert_ids = jnp.arange(expert_count, dtype=jnp.int32)
    slot_ids = jnp.arange(slot_count, dtype=jnp.int32)
    picked = (flat[None, None, :] == expert_ids[:, None, None]) & (rank[None, None, :] == slot_ids[None, :, None])
    return picked.astype(jnp.float32)


def expert_pass(pack):
    incoming_rows, incoming_output_gradient, hot_in, gate_w, up_weight_matrix, down_w, aup_w, up_adapter_weight, adown_w, down_adapter_weight = pack
    routing_mask = jnp.repeat(hot_in, RANK, axis=1)
    gate_pre = jnp.dot(incoming_rows, gate_w, preferred_element_type=jnp.float32)
    frozen_up_product = jnp.dot(incoming_rows, up_weight_matrix, preferred_element_type=jnp.float32)
    lowrank_input_rows = (jnp.dot(incoming_rows, aup_w, preferred_element_type=jnp.float32) * routing_mask).astype(jnp.bfloat16)
    combined_up_product = frozen_up_product + adapter_scale * jnp.dot(lowrank_input_rows, up_adapter_weight, preferred_element_type=jnp.float32)
    gate_act = jax.nn.silu(gate_pre)
    hidden = (gate_act * combined_up_product).astype(jnp.bfloat16)
    lowrank_cotangent = (jnp.dot(hidden, adown_w, preferred_element_type=jnp.float32) * routing_mask).astype(jnp.bfloat16)
    adapter_side_product = adapter_scale * jnp.dot(lowrank_cotangent, down_adapter_weight, preferred_element_type=jnp.float32)
    summed = jnp.dot(hidden, down_w, preferred_element_type=jnp.float32) + adapter_side_product
    expert_out = summed.astype(jnp.bfloat16)
    lowrank_down_gradient = (adapter_scale * jnp.dot(incoming_output_gradient, down_adapter_weight.T, preferred_element_type=jnp.float32) * routing_mask).astype(jnp.bfloat16)
    dhid_full = jnp.dot(incoming_output_gradient, down_w.T, preferred_element_type=jnp.float32) + jnp.dot(lowrank_down_gradient, adown_w.T, preferred_element_type=jnp.float32)
    hidden_gradient = (dhid_full * gate_act).astype(jnp.bfloat16)
    down_adapter_gradient = adapter_scale * jnp.dot(lowrank_cotangent.T, incoming_output_gradient, preferred_element_type=jnp.float32)
    grad_ad = jnp.dot(hidden.T, lowrank_down_gradient, preferred_element_type=jnp.float32)
    up_adapter_gradient = adapter_scale * jnp.dot(lowrank_input_rows.T, hidden_gradient, preferred_element_type=jnp.float32)
    lowrank_projected = adapter_scale * jnp.dot(hidden_gradient, up_adapter_weight.T, preferred_element_type=jnp.float32) * routing_mask
    grad_au = jnp.einsum('rd,rk->dk', incoming_rows.astype(jnp.float32), lowrank_projected, precision=lax.Precision.HIGHEST)
    return expert_out, grad_au, up_adapter_gradient, grad_ad, down_adapter_gradient


def reference(tokens, cotangent, routes, route_weight, tenant, w_gate, w_up, w_down, a_up, b_up, a_down, b_down):
    sources = N_DP
    tok_dev = tokens.reshape(sources, TOK_DEV, D)
    cot_dev = cotangent.reshape(sources, TOK_DEV, D)
    route_dev = routes.reshape(sources, TOK_DEV, TOP)
    weight_dev = route_weight.reshape(sources, TOK_DEV, TOP).astype(jnp.float32)
    tenant_dev = tenant.reshape(sources, TOK_DEV)
    slots = jax.vmap(lambda rows: slot_table(rows, EXPERTS, CAP))(route_dev)
    token_rep = jnp.repeat(tok_dev, TOP, axis=1).astype(jnp.float32)
    dout_rep = jnp.repeat(cot_dev, TOP, axis=1).astype(jnp.float32) * weight_dev.reshape(sources, TOK_DEV * TOP)[:, :, None]
    dout_rep = lax.optimization_barrier(dout_rep.astype(jnp.bfloat16)).astype(jnp.float32)
    tenant_hot = (tenant_dev[:, :, None] == jnp.arange(TENANTS, dtype=jnp.int32)[None, None, :]).astype(jnp.float32)
    hot_rep = jnp.repeat(tenant_hot, TOP, axis=1)
    slot_x = jnp.einsum('nesp,npd->nesd', slots, token_rep).astype(jnp.bfloat16)
    slot_do = jnp.einsum('nesp,npd->nesd', slots, dout_rep).astype(jnp.bfloat16)
    slot_hot = jnp.einsum('nesp,npt->nest', slots, hot_rep)
    rows_x = slot_x.transpose(1, 0, 2, 3).reshape(EXPERTS, sources * CAP, D)
    rows_do = slot_do.transpose(1, 0, 2, 3).reshape(EXPERTS, sources * CAP, D)
    rows_hot = slot_hot.transpose(1, 0, 2, 3).reshape(EXPERTS, sources * CAP, TENANTS)
    results = lax.map(expert_pass, (rows_x, rows_do, rows_hot, w_gate, w_up, w_down, a_up, b_up, a_down, b_down))
    expert_out, grad_a_up, grad_b_up, grad_a_down, grad_b_down = results
    back = expert_out.reshape(EXPERTS, sources, CAP, D).transpose(1, 0, 2, 3).astype(jnp.float32)
    picked = jnp.einsum('nesp,nesd->npd', slots, back)
    mixed = jnp.sum(picked.reshape(sources, TOK_DEV, TOP, D) * weight_dev[:, :, :, None], axis=2)
    mixed = mixed.reshape(TOKENS, D).astype(jnp.bfloat16)
    return mixed, grad_a_up, grad_b_up, grad_a_down, grad_b_down
```

```python
import functools

import jax
import jax.numpy as jnp
from jax import lax
from jax.experimental import pallas as pl
from jax.experimental.pallas import tpu as pltpu
from jax.sharding import PartitionSpec as P

TOP = 2
RANK = 32
TENANTS = 2
CAP = 64


adapter_scale = 0.5


def slot_table(route_rows, expert_count, slot_count):
    flat = route_rows.reshape(-1)
    order = jnp.arange(flat.shape[0], dtype=jnp.int32)
    earlier = (flat[:, None] == flat[None, :]) & (order[None, :] < order[:, None])
    rank = jnp.sum(earlier.astype(jnp.int32), axis=1)
    expert_ids = jnp.arange(expert_count, dtype=jnp.int32)
    slot_ids = jnp.arange(slot_count, dtype=jnp.int32)
    picked = (flat[None, None, :] == expert_ids[:, None, None]) & (
        rank[None, None, :] == slot_ids[None, :, None]
    )
    return picked.astype(jnp.bfloat16)


def on_device_plain(
    tokens,
    cotangent,
    routes,
    route_weight,
    tenant,
    w_gate,
    w_up,
    w_down,
    a_up,
    b_up,
    a_down,
    b_down,
):
    tok_count = tokens.shape[0]
    dwidth = tokens.shape[1]
    expert_count = lax.axis_size("dp")
    col_start = lax.axis_index("expert") * dwidth
    slot_pick = slot_table(routes, expert_count, CAP)
    token_rep = jnp.repeat(tokens, TOP, axis=0)
    dout_rep = (
        jnp.repeat(cotangent, TOP, axis=0).astype(jnp.float32) * route_weight.reshape(-1)[:, None]
    ).astype(jnp.bfloat16)
    tenant_hot = (tenant[:, None] == jnp.arange(TENANTS, dtype=jnp.int32)[None, :]).astype(
        jnp.bfloat16
    )
    hot_rep = jnp.repeat(tenant_hot, TOP, axis=0)
    send_x = jnp.einsum(
        "esp,pd->esd", slot_pick, token_rep, preferred_element_type=jnp.float32
    ).astype(jnp.bfloat16)
    send_do = jnp.einsum(
        "esp,pd->esd", slot_pick, dout_rep, preferred_element_type=jnp.float32
    ).astype(jnp.bfloat16)
    send_hot = jnp.einsum(
        "esp,pt->est", slot_pick, hot_rep, preferred_element_type=jnp.float32
    ).astype(jnp.bfloat16)
    got_x, got_do, got_hot = (
        lax.all_to_all(send_x, "dp", split_axis=0, concat_axis=0, tiled=True),
        lax.all_to_all(send_do, "dp", split_axis=0, concat_axis=0, tiled=True),
        lax.all_to_all(send_hot, "dp", split_axis=0, concat_axis=0, tiled=True),
    )
    local_rows = got_x.shape[0] * got_x.shape[1]
    rows_own = got_x.reshape(local_rows, dwidth)
    owned_output_gradient = got_do.reshape(local_rows, dwidth)
    hot_in = got_hot.reshape(local_rows, TENANTS)
    incoming_rows, incoming_output_gradient = (
        lax.all_gather(rows_own, "expert", axis=1, tiled=True),
        lax.all_gather(owned_output_gradient, "expert", axis=1, tiled=True),
    )
    gate_w = w_gate[0]
    up_weight_matrix = w_up[0]
    down_w = w_down[0]
    aup_w = a_up[0]
    up_adapter_weight = b_up[0]
    adown_w = a_down[0]
    down_adapter_weight = b_down[0]
    routing_mask = jnp.repeat(hot_in.astype(jnp.float32), RANK, axis=1)
    apart = jnp.dot(rows_own, aup_w, preferred_element_type=jnp.float32)
    partial_gradient = adapter_scale * jnp.dot(
        owned_output_gradient, down_adapter_weight.T, preferred_element_type=jnp.float32
    )
    a_total, d_total = lax.psum((apart, partial_gradient), "expert")
    lowrank_input_rows = (a_total * routing_mask).astype(jnp.bfloat16)
    lowrank_down_gradient = (d_total * routing_mask).astype(jnp.bfloat16)
    gate_pre = jnp.dot(incoming_rows, gate_w, preferred_element_type=jnp.float32)
    combined_up_product = jnp.dot(
        incoming_rows, up_weight_matrix, preferred_element_type=jnp.float32
    ) + adapter_scale * jnp.dot(
        lowrank_input_rows, up_adapter_weight, preferred_element_type=jnp.float32
    )
    gate_act = jax.nn.silu(gate_pre)
    hidden = (gate_act * combined_up_product).astype(jnp.bfloat16)
    c_total = lax.psum(jnp.dot(hidden, adown_w, preferred_element_type=jnp.float32), "expert")
    lowrank_cotangent = (c_total * routing_mask).astype(jnp.bfloat16)
    adapter_side_product = adapter_scale * jnp.dot(
        lowrank_cotangent, down_adapter_weight, preferred_element_type=jnp.float32
    )
    part = jnp.dot(hidden, down_w, preferred_element_type=jnp.float32)
    inner = lax.dynamic_slice_in_dim(part, col_start, dwidth, 1) + adapter_side_product
    whole_term = lax.dynamic_update_slice_in_dim(part, inner, col_start, 1)
    own_cols = lax.psum_scatter(whole_term, "expert", scatter_dimension=1, tiled=True).astype(
        jnp.bfloat16
    )
    back = lax.all_to_all(own_cols, "dp", split_axis=0, concat_axis=0, tiled=True)
    back = back.reshape(expert_count, CAP, dwidth)
    picked = jnp.einsum("esp,esd->pd", slot_pick, back, preferred_element_type=jnp.float32)
    mixed = jnp.sum(
        picked.reshape(tok_count, TOP, dwidth) * route_weight[:, :, None], axis=1
    ).astype(jnp.bfloat16)
    dhid_full = jnp.dot(
        incoming_output_gradient, down_w.T, preferred_element_type=jnp.float32
    ) + jnp.dot(lowrank_down_gradient, adown_w.T, preferred_element_type=jnp.float32)
    hidden_gradient = (dhid_full * gate_act).astype(jnp.bfloat16)
    down_adapter_gradient = adapter_scale * jnp.dot(
        lowrank_cotangent.T, owned_output_gradient, preferred_element_type=jnp.float32
    )
    grad_ad = jnp.dot(hidden.T, lowrank_down_gradient, preferred_element_type=jnp.float32)
    up_adapter_gradient = adapter_scale * jnp.dot(
        lowrank_input_rows.T, hidden_gradient, preferred_element_type=jnp.float32
    )
    projected_partial = (
        adapter_scale
        * jnp.dot(hidden_gradient, up_adapter_weight.T, preferred_element_type=jnp.float32)
        * routing_mask
    )
    projected = lax.psum(projected_partial, "expert")
    grad_au = jnp.einsum(
        "rd,rk->dk", rows_own.astype(jnp.float32), projected, precision=lax.Precision.HIGHEST
    )
    return (
        mixed,
        grad_au[None],
        up_adapter_gradient[None],
        grad_ad[None],
        down_adapter_gradient[None],
    )


NT = (((1,), (1,)), ((), ()))


def mm(a, b):
    return jnp.dot(a, b, preferred_element_type=jnp.float32)


def mm_nt(a, b):
    return lax.dot_general(a, b, NT, preferred_element_type=jnp.float32)


def fused_kernel(
    nz,
    nd,
    tok_ref,
    cot_ref,
    pick_ref,
    slotw_ref,
    tens_ref,
    c0_ref,
    c1_ref,
    rw_ref,
    wg_hbm,
    wu_hbm,
    wd_hbm,
    aupt_ref,
    bup_ref,
    adnt_ref,
    bdn_ref,
    mixed_ref,
    gaut_ref,
    gbu_ref,
    gadt_ref,
    gbd_ref,
    wg,
    wu,
    wd,
    tokg,
    cotg,
    selx,
    seld,
    xbuf,
    dbuf,
    gate,
    up,
    hidden,
    dhid,
    outs,
    back,
    mixs,
    mixr,
    mixo,
    tenr,
    part,
    wsem,
    zsend,
    zrecv,
    dsend,
    drecv,
    tsend,
    trecv,
    psend,
    precv,
    osend,
    orecv,
    msend,
    mrecv,
):
    z = lax.axis_index("expert")
    d = lax.axis_index("dp")
    width = tok_ref.shape[1]
    rows = nd * CAP
    ffl = gate.shape[1]
    tile = 512 if ffl % 512 == 0 else 256
    zs = [lax.rem(z + k, nz) for k in range(nz)]
    zb = [lax.rem(z - k + nz, nz) for k in range(nz)]
    ds_ = [lax.rem(d + k, nd) for k in range(nd)]
    db = [lax.rem(d - k + nd, nd) for k in range(nd)]
    pending = []

    def remote(src, dst, ssem, rsem, dev):
        return pltpu.make_async_remote_copy(
            src_ref=src,
            dst_ref=dst,
            send_sem=ssem,
            recv_sem=rsem,
            device_id=dev,
            device_id_type=pl.DeviceIdType.MESH,
        )

    def send(*args):
        copy = remote(*args)
        copy.start()
        pending.append(copy)

    def weight(i, s):
        lo = pl.multiple_of(s * width, width)
        if i == 0:
            return pltpu.make_async_copy(wg_hbm.at[0, pl.ds(lo, width), :], wg.at[s], wsem.at[i, s])
        if i == 1:
            return pltpu.make_async_copy(wu_hbm.at[0, pl.ds(lo, width), :], wu.at[s], wsem.at[i, s])
        return pltpu.make_async_copy(wd_hbm.at[0, :, pl.ds(lo, width)], wd.at[s], wsem.at[i, s])

    weight(0, z).start()
    weight(1, z).start()
    barrier = pltpu.get_barrier_semaphore()
    for k in range(1, nz):
        pl.semaphore_signal(
            barrier, inc=1, device_id={"expert": zs[k]}, device_id_type=pl.DeviceIdType.MESH
        )
    for k in range(1, nd):
        pl.semaphore_signal(
            barrier, inc=1, device_id={"dp": ds_[k]}, device_id_type=pl.DeviceIdType.MESH
        )
    pl.semaphore_wait(barrier, nz + nd - 2)

    for k in range(1, nz):
        send(tok_ref, tokg.at[z], zsend.at[0, k], zrecv.at[0, k], {"expert": zs[k]})
    for k in range(1, nd):
        send(tens_ref.at[ds_[k]], tenr.at[d], tsend.at[k], trecv.at[k], {"dp": ds_[k]})
    for k in range(1, nz):
        send(cot_ref, cotg.at[z], zsend.at[1, k], zrecv.at[1, k], {"expert": zs[k]})
    for k in range(1, nz):
        weight(0, zb[k]).start()
        weight(1, zb[k]).start()
    for k in range(nz):
        weight(2, zs[(k + 1) % nz]).start()

    def dispatch(which, j):
        s = zb[j]
        own, gathered, sel, buf = (
            (tok_ref, tokg, selx, xbuf) if which == 0 else (cot_ref, cotg, seld, dbuf)
        )
        if j:
            remote(
                own, gathered.at[s], zsend.at[which, j], zrecv.at[which, j], {"expert": zs[j]}
            ).wait_recv()
            block = gathered[s]
        else:
            block = own[...]
        for k in list(range(1, nd)) + [0]:
            e = ds_[k]
            picked = mm(pick_ref[e], block)
            if which:
                picked = picked * slotw_ref[e]
            picked = picked.astype(jnp.bfloat16)
            if k:
                sel[j, e] = picked
                send(
                    sel.at[j, e],
                    buf.at[s, d],
                    dsend.at[which, j, k],
                    drecv.at[which, j, k],
                    {"dp": e},
                )
            else:
                buf[s, d] = picked

    def arrived(which, j):
        s = zb[j]
        sel, buf = (selx, xbuf) if which == 0 else (seld, dbuf)
        for k in range(1, nd):
            remote(
                sel.at[j, ds_[k]],
                buf.at[s, db[k]],
                dsend.at[which, j, k],
                drecv.at[which, j, k],
                {"dp": ds_[k]},
            ).wait_recv()
        return s

    def part_out(kind, value):
        tot = jnp.where(ten() > 0.5, value[RANK:], value[:RANK])
        part[kind, z] = tot
        for k in range(1, nz):
            send(
                part.at[kind, z],
                part.at[kind, z],
                psend.at[kind, k],
                precv.at[kind, k],
                {"expert": zs[k]},
            )

    def part_in(kind, scale):
        for k in range(1, nz):
            remote(
                part.at[kind, z],
                part.at[kind, zb[k]],
                psend.at[kind, k],
                precv.at[kind, k],
                {"expert": zs[k]},
            ).wait_recv()
        tot = part[kind, 0]
        for i in range(1, nz):
            tot = tot + part[kind, i]
        tot = tot * scale
        high = ten() > 0.5
        return jnp.concatenate([jnp.where(high, 0.0, tot), jnp.where(high, tot, 0.0)], axis=0)

    def ten():
        tot = tenr[0, 0:1]
        for i in range(1, nd):
            tot = tot + tenr[i, 0:1]
        return tot

    def tiles(body):
        def run(i, carry):
            body(pl.ds(pl.multiple_of(i * tile, tile), tile))
            return carry

        lax.fori_loop(0, ffl // tile, run, 0)

    def forward(j):
        s = arrived(0, j)
        weight(0, s).wait()
        weight(1, s).wait()

        def body(cols):
            xs = xbuf[s].reshape(rows, width)
            g = mm(xs, wg[s, :, cols])
            u = mm(xs, wu[s, :, cols])
            if j:
                gate[:, cols] += g
                up[:, cols] += u
            else:
                gate[:, cols] = g
                up[:, cols] = u

        tiles(body)

    dispatch(0, 0)
    tenr[d] = tens_ref[d]
    for k in range(1, nd):
        remote(
            tens_ref.at[ds_[k]], tenr.at[db[k]], tsend.at[k], trecv.at[k], {"dp": ds_[k]}
        ).wait_recv()
    dispatch(0, 1)
    forward(0)
    part_out(0, mm_nt(aupt_ref[...], xbuf[z].reshape(rows, width)))
    for j in range(2, nz):
        dispatch(0, j)
        forward(j - 1)
    dispatch(1, 0)
    forward(nz - 1)
    low_a_t = part_in(0, 1.0)
    low_a = low_a_t.T.astype(jnp.bfloat16)
    low_a_t = low_a_t.astype(jnp.bfloat16)
    dispatch(1, 1)

    def act(cols):
        g = gate[:, cols]
        u = up[:, cols] + adapter_scale * mm(low_a, bup_ref[:, cols])
        a = g / (1.0 + jnp.exp(-g))
        gate[:, cols] = a
        hidden[:, cols] = (a * u).astype(jnp.bfloat16)

    tiles(act)
    part_out(2, mm_nt(adnt_ref[...], hidden[...]))
    dispatch(1, 2)

    def down(k, low_c):
        c = zs[k]
        weight(2, c).wait()
        for t in range(0, width, 256):
            n = min(256, width - t)
            r = mm(hidden[...], wd[c, :, t : t + n])
            if k == 0:
                r = r + adapter_scale * mm(low_c, bdn_ref[:, t : t + n])
            outs[c, :, :, t : t + n] = r.astype(jnp.bfloat16).reshape(nd, CAP, n)
        for i in range(1, nd):
            send(
                outs.at[c, ds_[i]], back.at[c, d], osend.at[k, i], orecv.at[k, i], {"dp": ds_[i]}
            )
        back[c, d] = outs[c, d]

    def combine(k):
        c = zs[k]
        for i in range(1, nd):
            remote(
                outs.at[c, ds_[i]], back.at[c, db[i]], osend.at[k, i], orecv.at[k, i], {"dp": ds_[i]}
            ).wait_recv()
        b = back[c].reshape(rows, width)
        m = mm(c0_ref[...], b) * rw_ref[:, 0:1] + mm(c1_ref[...], b) * rw_ref[:, 1:2]
        if k:
            mixs[c] = m.astype(jnp.bfloat16)
            send(mixs.at[c], mixr.at[z], msend.at[k], mrecv.at[k], {"expert": c})
        else:
            mixo[...] = m

    def backward(j, low_d):
        s = arrived(1, j) if j else z

        def body(cols):
            r = mm_nt(dbuf[s].reshape(rows, width), wd[s, cols, :])
            if j == 0:
                up[:, cols] = r
            elif j < nz - 1:
                up[:, cols] += r
            else:
                r = r + up[:, cols] + mm(low_d, adnt_ref[:, cols])
                dhid[:, cols] = (r * gate[:, cols]).astype(jnp.bfloat16)

        tiles(body)

    down(1, None)
    for j in range(3, nz):
        dispatch(1, j)
    for k in range(2, nz):
        down(k, None)
    low_c_t = part_in(2, 1.0)
    low_c = low_c_t.T.astype(jnp.bfloat16)
    down(0, low_c)
    arrived(1, 0)
    part_out(1, mm_nt(bdn_ref[...], dbuf[z].reshape(rows, width)))
    low_c_t = low_c_t.astype(jnp.bfloat16)
    combine(1)
    gbd_ref[...] = adapter_scale * mm(low_c_t, dbuf[z].reshape(rows, width))
    return_steps = list(range(2, nz)) + [0]
    low_d = None
    for j in range(nz):
        if j == nz - 1:
            low_d_t = part_in(1, adapter_scale)
            low_d = low_d_t.T.astype(jnp.bfloat16)
            low_d_t = low_d_t.astype(jnp.bfloat16)
        backward(j, low_d)
        if j < len(return_steps):
            combine(return_steps[j])
    part_out(3, mm_nt(bup_ref[...], dhid[...]))

    def grads(cols):
        gadt_ref[:, cols] = mm(low_d_t, hidden[:, cols])
        gbu_ref[:, cols] = adapter_scale * mm(low_a_t, dhid[:, cols])

    tiles(grads)
    low_z = part_in(3, adapter_scale)
    hi = low_z.astype(jnp.bfloat16)
    lo = (low_z - hi.astype(jnp.float32)).astype(jnp.bfloat16)
    xs = xbuf[z].reshape(rows, width)
    gaut_ref[...] = mm(hi, xs) + mm(lo, xs)
    total = mixo[...]
    for k in range(1, nz):
        remote(mixs.at[zs[k]], mixr.at[zb[k]], msend.at[k], mrecv.at[k], {"expert": zs[k]}).wait_recv()
        total = total + mixr[zb[k]].astype(jnp.float32)
    mixed_ref[...] = total.astype(jnp.bfloat16)
    for copy in pending:
        copy.wait_send()


def on_device_fused(
    tokens,
    cotangent,
    routes,
    route_weight,
    tenant,
    w_gate,
    w_up,
    w_down,
    a_up,
    b_up,
    a_down,
    b_down,
):
    nz, nd = lax.axis_size("expert"), lax.axis_size("dp")
    tok_count, width = tokens.shape
    ffl = w_gate.shape[2]
    rows = nd * CAP
    flat = routes.reshape(-1)
    order = jnp.arange(flat.shape[0], dtype=jnp.int32)
    earlier = (flat[:, None] == flat[None, :]) & (order[None, :] < order[:, None])
    rank = jnp.sum(earlier.astype(jnp.int32), axis=1)
    place = (flat * CAP + rank).reshape(tok_count, TOP)
    slot = jnp.arange(rows, dtype=jnp.int32)
    hit0 = place[None, :, 0] == slot[:, None]
    hit1 = place[None, :, 1] == slot[:, None]
    pick = (hit0 | hit1).astype(jnp.bfloat16).reshape(nd, CAP, tok_count)
    slotw = jnp.sum(
        jnp.where(hit0, route_weight[None, :, 0], 0.0)
        + jnp.where(hit1, route_weight[None, :, 1], 0.0),
        axis=1,
    ).reshape(nd, CAP, 1)
    slot_tenant = jnp.sum(
        jnp.where(hit0 | hit1, tenant[None, :].astype(jnp.float32), 0.0), axis=1
    ).reshape(nd, 1, 1, CAP)
    mine = (jnp.arange(nd, dtype=jnp.int32) == lax.axis_index("dp")).astype(jnp.float32)
    tens = jnp.broadcast_to(slot_tenant * mine[None, None, :, None], (nd, 8, nd, CAP)).reshape(
        nd, 8, rows
    )
    c0 = (place[:, 0:1] == slot[None, :]).astype(jnp.bfloat16)
    c1 = (place[:, 1:2] == slot[None, :]).astype(jnp.bfloat16)
    vmem = pl.BlockSpec(memory_space=pltpu.VMEM)
    hbm = pl.BlockSpec(memory_space=pl.ANY)
    bf, f32 = jnp.bfloat16, jnp.float32
    dma = pltpu.SemaphoreType.DMA
    wide = TENANTS * RANK
    mixed, gaut, gbu, gadt, gbd = pl.pallas_call(
        functools.partial(fused_kernel, nz, nd),
        out_shape=(
            jax.ShapeDtypeStruct((tok_count, width), bf),
            jax.ShapeDtypeStruct((wide, width), f32),
            jax.ShapeDtypeStruct((wide, ffl), f32),
            jax.ShapeDtypeStruct((wide, ffl), f32),
            jax.ShapeDtypeStruct((wide, width), f32),
        ),
        in_specs=[vmem] * 8 + [hbm] * 3 + [vmem] * 4,
        out_specs=[vmem] * 5,
        scratch_shapes=[
            pltpu.VMEM((nz, width, ffl), bf),
            pltpu.VMEM((nz, width, ffl), bf),
            pltpu.VMEM((nz, ffl, width), bf),
            pltpu.VMEM((nz, tok_count, width), bf),
            pltpu.VMEM((nz, tok_count, width), bf),
            pltpu.VMEM((nz, nd, CAP, width), bf),
            pltpu.VMEM((nz, nd, CAP, width), bf),
            pltpu.VMEM((nz, nd, CAP, width), bf),
            pltpu.VMEM((nz, nd, CAP, width), bf),
            pltpu.VMEM((rows, ffl), f32),
            pltpu.VMEM((rows, ffl), f32),
            pltpu.VMEM((rows, ffl), bf),
            pltpu.VMEM((rows, ffl), bf),
            pltpu.VMEM((nz, nd, CAP, width), bf),
            pltpu.VMEM((nz, nd, CAP, width), bf),
            pltpu.VMEM((nz, tok_count, width), bf),
            pltpu.VMEM((nz, tok_count, width), bf),
            pltpu.VMEM((tok_count, width), f32),
            pltpu.VMEM((nd, 8, rows), f32),
            pltpu.VMEM((4, nz, RANK, rows), f32),
            dma((3, nz)),
            dma((2, nz)),
            dma((2, nz)),
            dma((2, nz, nd)),
            dma((2, nz, nd)),
            dma((nd,)),
            dma((nd,)),
            dma((4, nz)),
            dma((4, nz)),
            dma((nz, nd)),
            dma((nz, nd)),
            dma((nz,)),
            dma((nz,)),
        ],
        compiler_params=pltpu.CompilerParams(
            collective_id=0, has_side_effects=True, vmem_limit_bytes=62 * 1024 * 1024
        ),
    )(
        tokens,
        cotangent,
        pick,
        slotw,
        tens,
        c0,
        c1,
        route_weight,
        w_gate,
        w_up,
        w_down,
        a_up[0].T,
        b_up[0],
        a_down[0].T,
        b_down[0],
    )
    return mixed, gaut.T[None], gbu[None], gadt.T[None], gbd[None]


def on_device(*args):
    nz, nd = lax.axis_size("expert"), lax.axis_size("dp")
    tok_count, width = args[0].shape
    ffl = args[5].shape[2]
    weight_bytes = 6 * nz * width * ffl
    row_bytes = 12 * nz * nd * CAP * width
    fits = weight_bytes + row_bytes <= 50 * 1024 * 1024
    if width % 128 or ffl % 256 or tok_count % 128 or (nd * CAP) % 128 or not fits:
        return on_device_plain(*args)
    return on_device_fused(*args)


def solution(mesh):
    return jax.shard_map(
        on_device,
        mesh=mesh,
        in_specs=(
            P(("groups", "dp"), "expert"),
            P(("groups", "dp"), "expert"),
            P(("groups", "dp"), None),
            P(("groups", "dp"), None),
            P(("groups", "dp")),
            P("dp", None, "expert"),
            P("dp", None, "expert"),
            P("dp", "expert", None),
            P("dp", "expert", None),
            P("dp", None, "expert"),
            P("dp", "expert", None),
            P("dp", None, "expert"),
        ),
        out_specs=(
            P(("groups", "dp"), "expert"),
            P(("groups", "dp"), "expert", None),
            P(("groups", "dp"), None, "expert"),
            P(("groups", "dp"), "expert", None),
            P(("groups", "dp"), None, "expert"),
        ),
        check_vma=False,
    )
```

```python
import functools

import jax
import jax.numpy as jnp
from jax import lax
from jax.experimental import pallas as pl
from jax.experimental.pallas import tpu as pltpu
from jax.sharding import PartitionSpec as P

TOP = 2
RANK = 32
TENANTS = 2
CAP = 64


adapter_scale = 0.5


def slot_table(route_rows, expert_count, slot_count):
    flat = route_rows.reshape(-1)
    order = jnp.arange(flat.shape[0], dtype=jnp.int32)
    earlier = (flat[:, None] == flat[None, :]) & (order[None, :] < order[:, None])
    rank = jnp.sum(earlier.astype(jnp.int32), axis=1)
    expert_ids = jnp.arange(expert_count, dtype=jnp.int32)
    slot_ids = jnp.arange(slot_count, dtype=jnp.int32)
    picked = (flat[None, None, :] == expert_ids[:, None, None]) & (
        rank[None, None, :] == slot_ids[None, :, None]
    )
    return picked.astype(jnp.bfloat16)


def on_device_plain(
    tokens,
    cotangent,
    routes,
    route_weight,
    tenant,
    w_gate,
    w_up,
    w_down,
    a_up,
    b_up,
    a_down,
    b_down,
):
    tok_count = tokens.shape[0]
    dwidth = tokens.shape[1]
    expert_count = lax.axis_size("dp")
    col_start = lax.axis_index("expert") * dwidth
    slot_pick = slot_table(routes, expert_count, CAP)
    token_rep = jnp.repeat(tokens, TOP, axis=0)
    dout_rep = (
        jnp.repeat(cotangent, TOP, axis=0).astype(jnp.float32) * route_weight.reshape(-1)[:, None]
    ).astype(jnp.bfloat16)
    tenant_hot = (tenant[:, None] == jnp.arange(TENANTS, dtype=jnp.int32)[None, :]).astype(
        jnp.bfloat16
    )
    hot_rep = jnp.repeat(tenant_hot, TOP, axis=0)
    send_x = jnp.einsum(
        "esp,pd->esd", slot_pick, token_rep, preferred_element_type=jnp.float32
    ).astype(jnp.bfloat16)
    send_do = jnp.einsum(
        "esp,pd->esd", slot_pick, dout_rep, preferred_element_type=jnp.float32
    ).astype(jnp.bfloat16)
    send_hot = jnp.einsum(
        "esp,pt->est", slot_pick, hot_rep, preferred_element_type=jnp.float32
    ).astype(jnp.bfloat16)
    got_x, got_do, got_hot = (
        lax.all_to_all(send_x, "dp", split_axis=0, concat_axis=0, tiled=True),
        lax.all_to_all(send_do, "dp", split_axis=0, concat_axis=0, tiled=True),
        lax.all_to_all(send_hot, "dp", split_axis=0, concat_axis=0, tiled=True),
    )
    local_rows = got_x.shape[0] * got_x.shape[1]
    rows_own = got_x.reshape(local_rows, dwidth)
    owned_output_gradient = got_do.reshape(local_rows, dwidth)
    hot_in = got_hot.reshape(local_rows, TENANTS)
    incoming_rows, incoming_output_gradient = (
        lax.all_gather(rows_own, "expert", axis=1, tiled=True),
        lax.all_gather(owned_output_gradient, "expert", axis=1, tiled=True),
    )
    gate_w = w_gate[0]
    up_weight_matrix = w_up[0]
    down_w = w_down[0]
    aup_w = a_up[0]
    up_adapter_weight = b_up[0]
    adown_w = a_down[0]
    down_adapter_weight = b_down[0]
    routing_mask = jnp.repeat(hot_in.astype(jnp.float32), RANK, axis=1)
    apart = jnp.dot(rows_own, aup_w, preferred_element_type=jnp.float32)
    partial_gradient = adapter_scale * jnp.dot(
        owned_output_gradient, down_adapter_weight.T, preferred_element_type=jnp.float32
    )
    a_total, d_total = lax.psum((apart, partial_gradient), "expert")
    lowrank_input_rows = (a_total * routing_mask).astype(jnp.bfloat16)
    lowrank_down_gradient = (d_total * routing_mask).astype(jnp.bfloat16)
    gate_pre = jnp.dot(incoming_rows, gate_w, preferred_element_type=jnp.float32)
    combined_up_product = jnp.dot(
        incoming_rows, up_weight_matrix, preferred_element_type=jnp.float32
    ) + adapter_scale * jnp.dot(
        lowrank_input_rows, up_adapter_weight, preferred_element_type=jnp.float32
    )
    gate_act = jax.nn.silu(gate_pre)
    hidden = (gate_act * combined_up_product).astype(jnp.bfloat16)
    c_total = lax.psum(jnp.dot(hidden, adown_w, preferred_element_type=jnp.float32), "expert")
    lowrank_cotangent = (c_total * routing_mask).astype(jnp.bfloat16)
    adapter_side_product = adapter_scale * jnp.dot(
        lowrank_cotangent, down_adapter_weight, preferred_element_type=jnp.float32
    )
    part = jnp.dot(hidden, down_w, preferred_element_type=jnp.float32)
    inner = lax.dynamic_slice_in_dim(part, col_start, dwidth, 1) + adapter_side_product
    whole_term = lax.dynamic_update_slice_in_dim(part, inner, col_start, 1)
    own_cols = lax.psum_scatter(whole_term, "expert", scatter_dimension=1, tiled=True).astype(
        jnp.bfloat16
    )
    back = lax.all_to_all(own_cols, "dp", split_axis=0, concat_axis=0, tiled=True)
    back = back.reshape(expert_count, CAP, dwidth)
    picked = jnp.einsum("esp,esd->pd", slot_pick, back, preferred_element_type=jnp.float32)
    mixed = jnp.sum(
        picked.reshape(tok_count, TOP, dwidth) * route_weight[:, :, None], axis=1
    ).astype(jnp.bfloat16)
    dhid_full = jnp.dot(
        incoming_output_gradient, down_w.T, preferred_element_type=jnp.float32
    ) + jnp.dot(lowrank_down_gradient, adown_w.T, preferred_element_type=jnp.float32)
    hidden_gradient = (dhid_full * gate_act).astype(jnp.bfloat16)
    down_adapter_gradient = adapter_scale * jnp.dot(
        lowrank_cotangent.T, owned_output_gradient, preferred_element_type=jnp.float32
    )
    grad_ad = jnp.dot(hidden.T, lowrank_down_gradient, preferred_element_type=jnp.float32)
    up_adapter_gradient = adapter_scale * jnp.dot(
        lowrank_input_rows.T, hidden_gradient, preferred_element_type=jnp.float32
    )
    projected_partial = (
        adapter_scale
        * jnp.dot(hidden_gradient, up_adapter_weight.T, preferred_element_type=jnp.float32)
        * routing_mask
    )
    projected = lax.psum(projected_partial, "expert")
    grad_au = jnp.einsum(
        "rd,rk->dk", rows_own.astype(jnp.float32), projected, precision=lax.Precision.HIGHEST
    )
    return (
        mixed,
        grad_au[None],
        up_adapter_gradient[None],
        grad_ad[None],
        down_adapter_gradient[None],
    )


NT = (((1,), (1,)), ((), ()))


def mm(a, b):
    return jnp.dot(a, b, preferred_element_type=jnp.float32)


def mm_nt(a, b):
    return lax.dot_general(a, b, NT, preferred_element_type=jnp.float32)


def fused_kernel(
    nz,
    nd,
    tok_ref,
    cot_ref,
    route_ref,
    rw_ref,
    tenant_ref,
    wg_hbm,
    wu_hbm,
    wd_hbm,
    aupt_ref,
    bup_ref,
    adnt_ref,
    bdn_ref,
    mixed_ref,
    gaut_ref,
    gbu_ref,
    gadt_ref,
    gbd_ref,
    pick_ref,
    slotw_ref,
    tens_ref,
    c0_ref,
    c1_ref,
    rwc_ref,
    wg,
    wu,
    wd,
    tokg,
    cotg,
    selx,
    seld,
    xbuf,
    dbuf,
    gate,
    up,
    hidden,
    dhid,
    outs,
    back,
    mixs,
    mixr,
    mixo,
    tenr,
    part,
    wsem,
    zsend,
    zrecv,
    dsend,
    drecv,
    tsend,
    trecv,
    psend,
    precv,
    osend,
    orecv,
    msend,
    mrecv,
):
    z = lax.axis_index("expert")
    d = lax.axis_index("dp")
    width = tok_ref.shape[1]
    rows = nd * CAP
    ffl = gate.shape[1]
    tile = 512 if ffl % 512 == 0 else 256
    zs = [lax.rem(z + k, nz) for k in range(nz)]
    zb = [lax.rem(z - k + nz, nz) for k in range(nz)]
    ds_ = [lax.rem(d + k, nd) for k in range(nd)]
    db = [lax.rem(d - k + nd, nd) for k in range(nd)]
    pending = []

    def remote(src, dst, ssem, rsem, dev):
        return pltpu.make_async_remote_copy(
            src_ref=src,
            dst_ref=dst,
            send_sem=ssem,
            recv_sem=rsem,
            device_id=dev,
            device_id_type=pl.DeviceIdType.MESH,
        )

    def send(*args):
        copy = remote(*args)
        copy.start()
        pending.append(copy)

    def weight(i, s):
        lo = pl.multiple_of(s * width, width)
        if i == 0:
            return pltpu.make_async_copy(wg_hbm.at[0, pl.ds(lo, width), :], wg.at[s], wsem.at[i, s])
        if i == 1:
            return pltpu.make_async_copy(wu_hbm.at[0, pl.ds(lo, width), :], wu.at[s], wsem.at[i, s])
        return pltpu.make_async_copy(wd_hbm.at[0, :, pl.ds(lo, width)], wd.at[s], wsem.at[i, s])

    weight(0, z).start()
    weight(1, z).start()
    barrier = pltpu.get_barrier_semaphore()
    for k in range(1, nz):
        pl.semaphore_signal(
            barrier, inc=1, device_id={"expert": zs[k]}, device_id_type=pl.DeviceIdType.MESH
        )
    for k in range(1, nd):
        pl.semaphore_signal(
            barrier, inc=1, device_id={"dp": ds_[k]}, device_id_type=pl.DeviceIdType.MESH
        )
    pl.semaphore_wait(barrier, nz + nd - 2)

    for k in range(1, nz):
        send(tok_ref, tokg.at[z], zsend.at[0, k], zrecv.at[0, k], {"expert": zs[k]})
    for k in range(1, nz):
        send(cot_ref, cotg.at[z], zsend.at[1, k], zrecv.at[1, k], {"expert": zs[k]})
    for k in range(1, nz):
        weight(0, zb[k]).start()
        weight(1, zb[k]).start()
    for k in range(nz):
        weight(2, zs[(k + 1) % nz]).start()

    toks = tok_ref.shape[0]
    f32, bf = jnp.float32, jnp.bfloat16
    lane = lax.broadcasted_iota(jnp.int32, (toks, toks), 1)
    line = lax.broadcasted_iota(jnp.int32, (toks, toks), 0)
    sooner = jnp.where(line < lane, 1.0, 0.0).astype(bf)
    expert_id = lax.broadcasted_iota(jnp.int32, (toks, toks), 0)
    hot = [jnp.where(expert_id == route_ref[k : k + 1, :], 1.0, 0.0) for k in range(TOP)]
    count = mm(sum(hot).astype(bf), sooner)
    slot_id = lax.broadcasted_iota(jnp.int32, (rows, toks), 0).astype(f32)
    hits, slot_weight = [], 0.0
    for k in range(TOP):
        rank = jnp.sum(hot[k] * count, axis=0, keepdims=True)
        place = route_ref[k : k + 1, :].astype(f32) * CAP + rank
        hit = jnp.where((slot_id == place), 1.0, 0.0)
        hits.append(hit)
        weights = rw_ref[k : k + 1, :]
        slot_weight = slot_weight + jnp.sum(hit * weights, axis=1, keepdims=True)
        c_ref = (c0_ref, c1_ref)[k]
        c_ref[...] = hit.T.astype(bf)
        rwc_ref[k] = jnp.broadcast_to(weights, (toks, toks)).T
    pick = (hits[0] + hits[1]).astype(bf)
    pick_ref[...] = pick.reshape(nd, CAP, toks)
    slotw_ref[...] = jnp.broadcast_to(slot_weight, (rows, toks)).reshape(nd, CAP, toks)
    tenant_row = jnp.broadcast_to(tenant_ref[...].astype(f32), (8, toks)).astype(bf)
    slot_tenant = mm(tenant_row, c0_ref[...]) + mm(tenant_row, c1_ref[...])
    slot_lane = lax.broadcasted_iota(jnp.int32, (8, rows), 1)
    mine = (slot_lane >= d * CAP) & (slot_lane < (d + 1) * CAP)
    for k in range(nd):
        turned = slot_tenant if k == 0 else pltpu.roll(slot_tenant, (nd - k) * CAP, 1)
        tens_ref[k] = jnp.where(mine, turned, 0.0)
    for k in range(1, nd):
        send(tens_ref.at[k], tenr.at[d], tsend.at[k], trecv.at[k], {"dp": ds_[k]})

    def dispatch(which, j):
        s = zb[j]
        own, gathered, sel, buf = (
            (tok_ref, tokg, selx, xbuf) if which == 0 else (cot_ref, cotg, seld, dbuf)
        )
        if j:
            remote(
                own, gathered.at[s], zsend.at[which, j], zrecv.at[which, j], {"expert": zs[j]}
            ).wait_recv()
            block = gathered[s]
        else:
            block = own[...]
        for k in list(range(1, nd)) + [0]:
            e = ds_[k]
            picked = mm(pick_ref[e], block)
            if which:
                picked = picked * slotw_ref[e, :, 0:1]
            picked = picked.astype(jnp.bfloat16)
            if k:
                sel[j, e] = picked
                send(
                    sel.at[j, e],
                    buf.at[s, d],
                    dsend.at[which, j, k],
                    drecv.at[which, j, k],
                    {"dp": e},
                )
            else:
                buf[s, d] = picked

    def arrived(which, j):
        s = zb[j]
        sel, buf = (selx, xbuf) if which == 0 else (seld, dbuf)
        for k in range(1, nd):
            remote(
                sel.at[j, ds_[k]],
                buf.at[s, db[k]],
                dsend.at[which, j, k],
                drecv.at[which, j, k],
                {"dp": ds_[k]},
            ).wait_recv()
        return s

    def part_out(kind, value):
        tot = jnp.where(ten() > 0.5, value[RANK:], value[:RANK])
        part[kind, z] = tot
        for k in range(1, nz):
            send(
                part.at[kind, z],
                part.at[kind, z],
                psend.at[kind, k],
                precv.at[kind, k],
                {"expert": zs[k]},
            )

    def part_in(kind, scale):
        for k in range(1, nz):
            remote(
                part.at[kind, z],
                part.at[kind, zb[k]],
                psend.at[kind, k],
                precv.at[kind, k],
                {"expert": zs[k]},
            ).wait_recv()
        tot = part[kind, 0]
        for i in range(1, nz):
            tot = tot + part[kind, i]
        tot = tot * scale
        high = ten() > 0.5
        return jnp.concatenate([jnp.where(high, 0.0, tot), jnp.where(high, tot, 0.0)], axis=0)

    def ten():
        tot = tenr[0, 0:1]
        for i in range(1, nd):
            tot = tot + tenr[i, 0:1]
        return tot

    def tiles(body):
        def run(i, carry):
            body(pl.ds(pl.multiple_of(i * tile, tile), tile))
            return carry

        lax.fori_loop(0, ffl // tile, run, 0)

    def forward(j):
        s = arrived(0, j)
        weight(0, s).wait()
        weight(1, s).wait()

        def body(cols):
            xs = xbuf[s].reshape(rows, width)
            g = mm(xs, wg[s, :, cols])
            u = mm(xs, wu[s, :, cols])
            if j:
                gate[:, cols] += g
                up[:, cols] += u
            else:
                gate[:, cols] = g
                up[:, cols] = u

        tiles(body)

    dispatch(0, 0)
    tenr[d] = tens_ref[0]
    for k in range(1, nd):
        remote(
            tens_ref.at[k], tenr.at[db[k]], tsend.at[k], trecv.at[k], {"dp": ds_[k]}
        ).wait_recv()
    dispatch(0, 1)
    forward(0)
    part_out(0, mm_nt(aupt_ref[...], xbuf[z].reshape(rows, width)))
    for j in range(2, nz):
        dispatch(0, j)
        forward(j - 1)
    dispatch(1, 0)
    forward(nz - 1)
    low_a_t = part_in(0, 1.0)
    low_a = low_a_t.T.astype(jnp.bfloat16)
    low_a_t = low_a_t.astype(jnp.bfloat16)
    dispatch(1, 1)

    def act(cols):
        g = gate[:, cols]
        u = up[:, cols] + adapter_scale * mm(low_a, bup_ref[:, cols])
        a = g / (1.0 + jnp.exp(-g))
        gate[:, cols] = a
        hidden[:, cols] = (a * u).astype(jnp.bfloat16)

    tiles(act)
    part_out(2, mm_nt(adnt_ref[...], hidden[...]))
    dispatch(1, 2)

    def down(k, low_c):
        c = zs[k]
        weight(2, c).wait()
        for t in range(0, width, 256):
            n = min(256, width - t)
            r = mm(hidden[...], wd[c, :, t : t + n])
            if k == 0:
                r = r + adapter_scale * mm(low_c, bdn_ref[:, t : t + n])
            outs[c, :, :, t : t + n] = r.astype(jnp.bfloat16).reshape(nd, CAP, n)
        for i in range(1, nd):
            send(
                outs.at[c, ds_[i]], back.at[c, d], osend.at[k, i], orecv.at[k, i], {"dp": ds_[i]}
            )
        back[c, d] = outs[c, d]

    def combine(k):
        c = zs[k]
        for i in range(1, nd):
            remote(
                outs.at[c, ds_[i]], back.at[c, db[i]], osend.at[k, i], orecv.at[k, i], {"dp": ds_[i]}
            ).wait_recv()
        b = back[c].reshape(rows, width)
        m = mm(c0_ref[...], b) * rwc_ref[0, :, 0:1] + mm(c1_ref[...], b) * rwc_ref[1, :, 0:1]
        if k:
            mixs[c] = m.astype(jnp.bfloat16)
            send(mixs.at[c], mixr.at[z], msend.at[k], mrecv.at[k], {"expert": c})
        else:
            mixo[...] = m

    def backward(j, low_d):
        s = arrived(1, j) if j else z

        def body(cols):
            r = mm_nt(dbuf[s].reshape(rows, width), wd[s, cols, :])
            if j == 0:
                up[:, cols] = r
            elif j < nz - 1:
                up[:, cols] += r
            else:
                r = r + up[:, cols] + mm(low_d, adnt_ref[:, cols])
                dhid[:, cols] = (r * gate[:, cols]).astype(jnp.bfloat16)

        tiles(body)

    down(1, None)
    for j in range(3, nz):
        dispatch(1, j)
    for k in range(2, nz):
        down(k, None)
    low_c_t = part_in(2, 1.0)
    low_c = low_c_t.T.astype(jnp.bfloat16)
    down(0, low_c)
    arrived(1, 0)
    part_out(1, mm_nt(bdn_ref[...], dbuf[z].reshape(rows, width)))
    low_c_t = low_c_t.astype(jnp.bfloat16)
    combine(1)
    gbd_ref[...] = adapter_scale * mm(low_c_t, dbuf[z].reshape(rows, width))
    return_steps = list(range(2, nz)) + [0]
    low_d = None
    for j in range(nz):
        if j == nz - 1:
            low_d_t = part_in(1, adapter_scale)
            low_d = low_d_t.T.astype(jnp.bfloat16)
            low_d_t = low_d_t.astype(jnp.bfloat16)
        backward(j, low_d)
        if j < len(return_steps):
            combine(return_steps[j])
    part_out(3, mm_nt(bup_ref[...], dhid[...]))

    def grads(cols):
        gadt_ref[:, cols] = mm(low_d_t, hidden[:, cols])
        gbu_ref[:, cols] = adapter_scale * mm(low_a_t, dhid[:, cols])

    tiles(grads)
    low_z = part_in(3, adapter_scale)
    hi = low_z.astype(jnp.bfloat16)
    lo = (low_z - hi.astype(jnp.float32)).astype(jnp.bfloat16)
    xs = xbuf[z].reshape(rows, width)
    gaut_ref[...] = mm(hi, xs) + mm(lo, xs)
    total = mixo[...]
    for k in range(1, nz):
        remote(mixs.at[zs[k]], mixr.at[zb[k]], msend.at[k], mrecv.at[k], {"expert": zs[k]}).wait_recv()
        total = total + mixr[zb[k]].astype(jnp.float32)
    mixed_ref[...] = total.astype(jnp.bfloat16)
    for copy in pending:
        copy.wait_send()


def hand_over(*refs):
    sems = refs[-1]
    half = len(refs) // 2
    copies = [
        pltpu.make_async_copy(refs[i], refs[half + i], sems.at[i]) for i in range(half)
    ]
    for copy in copies:
        copy.start()
    for copy in copies:
        copy.wait()


def on_device_fused(
    tokens,
    cotangent,
    routes,
    route_weight,
    tenant,
    w_gate,
    w_up,
    w_down,
    a_up,
    b_up,
    a_down,
    b_down,
):
    nz, nd = lax.axis_size("expert"), lax.axis_size("dp")
    tok_count, width = tokens.shape
    ffl = w_gate.shape[2]
    rows = nd * CAP
    vmem = pl.BlockSpec(memory_space=pltpu.VMEM)
    hbm = pl.BlockSpec(memory_space=pl.ANY)
    bf, f32 = jnp.bfloat16, jnp.float32
    dma = pltpu.SemaphoreType.DMA
    wide = TENANTS * RANK
    results = pl.pallas_call(
        functools.partial(fused_kernel, nz, nd),
        out_shape=(
            jax.ShapeDtypeStruct((tok_count, width), bf),
            jax.ShapeDtypeStruct((wide, width), f32),
            jax.ShapeDtypeStruct((wide, ffl), f32),
            jax.ShapeDtypeStruct((wide, ffl), f32),
            jax.ShapeDtypeStruct((wide, width), f32),
        ),
        in_specs=[vmem] * 5 + [hbm] * 3 + [vmem] * 4,
        out_specs=[vmem] * 5,
        scratch_shapes=[
            pltpu.VMEM((nd, CAP, tok_count), bf),
            pltpu.VMEM((nd, CAP, tok_count), f32),
            pltpu.VMEM((nd, 8, rows), f32),
            pltpu.VMEM((tok_count, rows), bf),
            pltpu.VMEM((tok_count, rows), bf),
            pltpu.VMEM((TOP, tok_count, tok_count), f32),
            pltpu.VMEM((nz, width, ffl), bf),
            pltpu.VMEM((nz, width, ffl), bf),
            pltpu.VMEM((nz, ffl, width), bf),
            pltpu.VMEM((nz, tok_count, width), bf),
            pltpu.VMEM((nz, tok_count, width), bf),
            pltpu.VMEM((nz, nd, CAP, width), bf),
            pltpu.VMEM((nz, nd, CAP, width), bf),
            pltpu.VMEM((nz, nd, CAP, width), bf),
            pltpu.VMEM((nz, nd, CAP, width), bf),
            pltpu.VMEM((rows, ffl), f32),
            pltpu.VMEM((rows, ffl), f32),
            pltpu.VMEM((rows, ffl), bf),
            pltpu.VMEM((rows, ffl), bf),
            pltpu.VMEM((nz, nd, CAP, width), bf),
            pltpu.VMEM((nz, nd, CAP, width), bf),
            pltpu.VMEM((nz, tok_count, width), bf),
            pltpu.VMEM((nz, tok_count, width), bf),
            pltpu.VMEM((tok_count, width), f32),
            pltpu.VMEM((nd, 8, rows), f32),
            pltpu.VMEM((4, nz, RANK, rows), f32),
            dma((3, nz)),
            dma((2, nz)),
            dma((2, nz)),
            dma((2, nz, nd)),
            dma((2, nz, nd)),
            dma((nd,)),
            dma((nd,)),
            dma((4, nz)),
            dma((4, nz)),
            dma((nz, nd)),
            dma((nz, nd)),
            dma((nz,)),
            dma((nz,)),
        ],
        compiler_params=pltpu.CompilerParams(
            collective_id=0, has_side_effects=True, vmem_limit_bytes=62 * 1024 * 1024
        ),
    )(
        tokens,
        cotangent,
        routes.T,
        route_weight.T,
        tenant[None],
        w_gate,
        w_up,
        w_down,
        a_up[0].T,
        b_up[0],
        a_down[0].T,
        b_down[0],
    )
    count = len(results)
    mixed, gaut, gbu, gadt, gbd = pl.pallas_call(
        hand_over,
        out_shape=tuple(jax.ShapeDtypeStruct(r.shape, r.dtype) for r in results),
        in_specs=[hbm] * count,
        out_specs=[hbm] * count,
        scratch_shapes=[dma((count,))],
        compiler_params=pltpu.CompilerParams(vmem_limit_bytes=60 * 1024 * 1024),
    )(*results)
    return mixed, gaut.T[None], gbu[None], gadt.T[None], gbd[None]


def on_device(*args):
    nz, nd = lax.axis_size("expert"), lax.axis_size("dp")
    tok_count, width = args[0].shape
    ffl = args[5].shape[2]
    weight_bytes = 6 * nz * width * ffl
    row_bytes = 12 * nz * nd * CAP * width
    fits = weight_bytes + row_bytes <= 50 * 1024 * 1024
    if width % 128 or ffl % 256 or tok_count % 128 or (nd * CAP) % 128 or not fits:
        return on_device_plain(*args)
    return on_device_fused(*args)


def solution(mesh):
    return jax.shard_map(
        on_device,
        mesh=mesh,
        in_specs=(
            P(("groups", "dp"), "expert"),
            P(("groups", "dp"), "expert"),
            P(("groups", "dp"), None),
            P(("groups", "dp"), None),
            P(("groups", "dp")),
            P("dp", None, "expert"),
            P("dp", None, "expert"),
            P("dp", "expert", None),
            P("dp", "expert", None),
            P("dp", None, "expert"),
            P("dp", "expert", None),
            P("dp", None, "expert"),
        ),
        out_specs=(
            P(("groups", "dp"), "expert"),
            P(("groups", "dp"), "expert", None),
            P(("groups", "dp"), None, "expert"),
            P(("groups", "dp"), "expert", None),
            P(("groups", "dp"), None, "expert"),
        ),
        check_vma=False,
    )
```

```python
import functools

import jax
import jax.numpy as jnp
from jax import lax
from jax.experimental import pallas as pl
from jax.experimental.pallas import tpu as pltpu
from jax.sharding import PartitionSpec as P

TOP = 2
RANK = 32
TENANTS = 2
CAP = 64


adapter_scale = 0.5


def slot_table(route_rows, expert_count, slot_count):
    flat = route_rows.reshape(-1)
    order = jnp.arange(flat.shape[0], dtype=jnp.int32)
    earlier = (flat[:, None] == flat[None, :]) & (order[None, :] < order[:, None])
    rank = jnp.sum(earlier.astype(jnp.int32), axis=1)
    expert_ids = jnp.arange(expert_count, dtype=jnp.int32)
    slot_ids = jnp.arange(slot_count, dtype=jnp.int32)
    picked = (flat[None, None, :] == expert_ids[:, None, None]) & (
        rank[None, None, :] == slot_ids[None, :, None]
    )
    return picked.astype(jnp.bfloat16)


def on_device_plain(
    tokens,
    cotangent,
    routes,
    route_weight,
    tenant,
    w_gate,
    w_up,
    w_down,
    a_up,
    b_up,
    a_down,
    b_down,
):
    tok_count = tokens.shape[0]
    dwidth = tokens.shape[1]
    expert_count = lax.axis_size("dp")
    col_start = lax.axis_index("expert") * dwidth
    slot_pick = slot_table(routes, expert_count, CAP)
    token_rep = jnp.repeat(tokens, TOP, axis=0)
    dout_rep = (
        jnp.repeat(cotangent, TOP, axis=0).astype(jnp.float32) * route_weight.reshape(-1)[:, None]
    ).astype(jnp.bfloat16)
    tenant_hot = (tenant[:, None] == jnp.arange(TENANTS, dtype=jnp.int32)[None, :]).astype(
        jnp.bfloat16
    )
    hot_rep = jnp.repeat(tenant_hot, TOP, axis=0)
    send_x = jnp.einsum(
        "esp,pd->esd", slot_pick, token_rep, preferred_element_type=jnp.float32
    ).astype(jnp.bfloat16)
    send_do = jnp.einsum(
        "esp,pd->esd", slot_pick, dout_rep, preferred_element_type=jnp.float32
    ).astype(jnp.bfloat16)
    send_hot = jnp.einsum(
        "esp,pt->est", slot_pick, hot_rep, preferred_element_type=jnp.float32
    ).astype(jnp.bfloat16)
    got_x, got_do, got_hot = (
        lax.all_to_all(send_x, "dp", split_axis=0, concat_axis=0, tiled=True),
        lax.all_to_all(send_do, "dp", split_axis=0, concat_axis=0, tiled=True),
        lax.all_to_all(send_hot, "dp", split_axis=0, concat_axis=0, tiled=True),
    )
    local_rows = got_x.shape[0] * got_x.shape[1]
    rows_own = got_x.reshape(local_rows, dwidth)
    owned_output_gradient = got_do.reshape(local_rows, dwidth)
    hot_in = got_hot.reshape(local_rows, TENANTS)
    incoming_rows, incoming_output_gradient = (
        lax.all_gather(rows_own, "expert", axis=1, tiled=True),
        lax.all_gather(owned_output_gradient, "expert", axis=1, tiled=True),
    )
    gate_w = w_gate[0]
    up_weight_matrix = w_up[0]
    down_w = w_down[0]
    aup_w = a_up[0]
    up_adapter_weight = b_up[0]
    adown_w = a_down[0]
    down_adapter_weight = b_down[0]
    routing_mask = jnp.repeat(hot_in.astype(jnp.float32), RANK, axis=1)
    apart = jnp.dot(rows_own, aup_w, preferred_element_type=jnp.float32)
    partial_gradient = adapter_scale * jnp.dot(
        owned_output_gradient, down_adapter_weight.T, preferred_element_type=jnp.float32
    )
    a_total, d_total = lax.psum((apart, partial_gradient), "expert")
    lowrank_input_rows = (a_total * routing_mask).astype(jnp.bfloat16)
    lowrank_down_gradient = (d_total * routing_mask).astype(jnp.bfloat16)
    gate_pre = jnp.dot(incoming_rows, gate_w, preferred_element_type=jnp.float32)
    combined_up_product = jnp.dot(
        incoming_rows, up_weight_matrix, preferred_element_type=jnp.float32
    ) + adapter_scale * jnp.dot(
        lowrank_input_rows, up_adapter_weight, preferred_element_type=jnp.float32
    )
    gate_act = jax.nn.silu(gate_pre)
    hidden = (gate_act * combined_up_product).astype(jnp.bfloat16)
    c_total = lax.psum(jnp.dot(hidden, adown_w, preferred_element_type=jnp.float32), "expert")
    lowrank_cotangent = (c_total * routing_mask).astype(jnp.bfloat16)
    adapter_side_product = adapter_scale * jnp.dot(
        lowrank_cotangent, down_adapter_weight, preferred_element_type=jnp.float32
    )
    part = jnp.dot(hidden, down_w, preferred_element_type=jnp.float32)
    inner = lax.dynamic_slice_in_dim(part, col_start, dwidth, 1) + adapter_side_product
    whole_term = lax.dynamic_update_slice_in_dim(part, inner, col_start, 1)
    own_cols = lax.psum_scatter(whole_term, "expert", scatter_dimension=1, tiled=True).astype(
        jnp.bfloat16
    )
    back = lax.all_to_all(own_cols, "dp", split_axis=0, concat_axis=0, tiled=True)
    back = back.reshape(expert_count, CAP, dwidth)
    picked = jnp.einsum("esp,esd->pd", slot_pick, back, preferred_element_type=jnp.float32)
    mixed = jnp.sum(
        picked.reshape(tok_count, TOP, dwidth) * route_weight[:, :, None], axis=1
    ).astype(jnp.bfloat16)
    dhid_full = jnp.dot(
        incoming_output_gradient, down_w.T, preferred_element_type=jnp.float32
    ) + jnp.dot(lowrank_down_gradient, adown_w.T, preferred_element_type=jnp.float32)
    hidden_gradient = (dhid_full * gate_act).astype(jnp.bfloat16)
    down_adapter_gradient = adapter_scale * jnp.dot(
        lowrank_cotangent.T, owned_output_gradient, preferred_element_type=jnp.float32
    )
    grad_ad = jnp.dot(hidden.T, lowrank_down_gradient, preferred_element_type=jnp.float32)
    up_adapter_gradient = adapter_scale * jnp.dot(
        lowrank_input_rows.T, hidden_gradient, preferred_element_type=jnp.float32
    )
    projected_partial = (
        adapter_scale
        * jnp.dot(hidden_gradient, up_adapter_weight.T, preferred_element_type=jnp.float32)
        * routing_mask
    )
    projected = lax.psum(projected_partial, "expert")
    grad_au = jnp.einsum(
        "rd,rk->dk", rows_own.astype(jnp.float32), projected, precision=lax.Precision.HIGHEST
    )
    return (
        mixed,
        grad_au[None],
        up_adapter_gradient[None],
        grad_ad[None],
        down_adapter_gradient[None],
    )


NT = (((1,), (1,)), ((), ()))


def mm(a, b):
    return jnp.dot(a, b, preferred_element_type=jnp.float32)


def mm_nt(a, b):
    return lax.dot_general(a, b, NT, preferred_element_type=jnp.float32)


def fused_kernel(
    nz,
    nd,
    tok_ref,
    cot_ref,
    route_ref,
    rw_ref,
    tenant_ref,
    wg_hbm,
    wu_hbm,
    wd_hbm,
    aupt_ref,
    bup_ref,
    adnt_ref,
    bdn_ref,
    mixed_ref,
    gaut_ref,
    gbu_ref,
    gadt_ref,
    gbd_ref,
    pick_ref,
    slotw_ref,
    tens_ref,
    c0_ref,
    c1_ref,
    rwc_ref,
    wg,
    wu,
    wd,
    tokg,
    cotg,
    selx,
    seld,
    xbuf,
    dbuf,
    gate,
    up,
    hidden,
    dhid,
    outs,
    back,
    mixs,
    mixr,
    mixo,
    tenr,
    part,
    wsem,
    zsend,
    zrecv,
    dsend,
    drecv,
    tsend,
    trecv,
    psend,
    precv,
    osend,
    orecv,
    msend,
    mrecv,
):
    z = lax.axis_index("expert")
    d = lax.axis_index("dp")
    width = tok_ref.shape[1]
    rows = nd * CAP
    ffl = gate.shape[1]
    tile = 512 if ffl % 512 == 0 else 256
    zs = [lax.rem(z + k, nz) for k in range(nz)]
    zb = [lax.rem(z - k + nz, nz) for k in range(nz)]
    ds_ = [lax.rem(d + k, nd) for k in range(nd)]
    db = [lax.rem(d - k + nd, nd) for k in range(nd)]
    pending = []
    below, above = z, nz - 1 - z
    both = jnp.minimum(below, above)
    longer = jnp.where(below > above, -1, 1)
    near = [z]
    for k in range(1, nz):
        paired = (1 if k % 2 else -1) * ((k + 1) // 2)
        near.append(z + jnp.where(k <= 2 * both, paired, longer * (k - both)))

    def remote(src, dst, ssem, rsem, dev):
        return pltpu.make_async_remote_copy(
            src_ref=src,
            dst_ref=dst,
            send_sem=ssem,
            recv_sem=rsem,
            device_id=dev,
            device_id_type=pl.DeviceIdType.MESH,
        )

    def send(*args):
        copy = remote(*args)
        copy.start()
        pending.append(copy)

    def weight(i, s):
        lo = pl.multiple_of(s * width, width)
        if i == 0:
            return pltpu.make_async_copy(wg_hbm.at[0, pl.ds(lo, width), :], wg.at[s], wsem.at[i, s])
        if i == 1:
            return pltpu.make_async_copy(wu_hbm.at[0, pl.ds(lo, width), :], wu.at[s], wsem.at[i, s])
        return pltpu.make_async_copy(wd_hbm.at[0, :, pl.ds(lo, width)], wd.at[s], wsem.at[i, s])

    weight(0, z).start()
    weight(1, z).start()
    barrier = pltpu.get_barrier_semaphore()
    for k in range(1, nz):
        pl.semaphore_signal(
            barrier, inc=1, device_id={"expert": zs[k]}, device_id_type=pl.DeviceIdType.MESH
        )
    for k in range(1, nd):
        pl.semaphore_signal(
            barrier, inc=1, device_id={"dp": ds_[k]}, device_id_type=pl.DeviceIdType.MESH
        )
    pl.semaphore_wait(barrier, nz + nd - 2)

    line_sends = []

    def line_send(src, dst, which, s, up_way, may):
        copy = remote(
            src,
            dst,
            zsend.at[which, s, up_way],
            zrecv.at[which, s],
            {"expert": lax.rem(z + nz + 2 * up_way - 1, nz)},
        )
        line_sends.append((copy, may))
        pl.when(may)(copy.start)

    def own_line(which):
        own, gathered = ((tok_ref, tokg), (cot_ref, cotg))[which]
        line_send(own, gathered.at[z], which, z, 0, z > 0)
        line_send(own, gathered.at[z], which, z, 1, z < nz - 1)

    own_line(0)

    for k in range(1, nz):
        weight(0, near[k]).start()
        weight(1, near[k]).start()
    for k in range(nz):
        weight(2, zs[(k + 1) % nz]).start()

    toks = tok_ref.shape[0]
    f32, bf = jnp.float32, jnp.bfloat16
    lane = lax.broadcasted_iota(jnp.int32, (toks, toks), 1)
    line = lax.broadcasted_iota(jnp.int32, (toks, toks), 0)
    sooner = jnp.where(line < lane, 1.0, 0.0).astype(bf)
    expert_id = lax.broadcasted_iota(jnp.int32, (toks, toks), 0)
    hot = [jnp.where(expert_id == route_ref[k : k + 1, :], 1.0, 0.0) for k in range(TOP)]
    count = mm(sum(hot).astype(bf), sooner)
    slot_id = lax.broadcasted_iota(jnp.int32, (rows, toks), 0).astype(f32)
    hits, slot_weight = [], 0.0
    for k in range(TOP):
        rank = jnp.sum(hot[k] * count, axis=0, keepdims=True)
        place = route_ref[k : k + 1, :].astype(f32) * CAP + rank
        hit = jnp.where((slot_id == place), 1.0, 0.0)
        hits.append(hit)
        weights = rw_ref[k : k + 1, :]
        slot_weight = slot_weight + jnp.sum(hit * weights, axis=1, keepdims=True)
        c_ref = (c0_ref, c1_ref)[k]
        c_ref[...] = hit.T.astype(bf)
        rwc_ref[k] = jnp.broadcast_to(weights, (toks, toks)).T
    pick = (hits[0] + hits[1]).astype(bf)
    pick_ref[...] = pick.reshape(nd, CAP, toks)
    slotw_ref[...] = jnp.broadcast_to(slot_weight, (rows, toks)).reshape(nd, CAP, toks)
    tenant_row = jnp.broadcast_to(tenant_ref[...].astype(f32), (8, toks)).astype(bf)
    slot_tenant = mm(tenant_row, c0_ref[...]) + mm(tenant_row, c1_ref[...])
    slot_lane = lax.broadcasted_iota(jnp.int32, (8, rows), 1)
    mine = (slot_lane >= d * CAP) & (slot_lane < (d + 1) * CAP)
    for k in range(nd):
        turned = slot_tenant if k == 0 else pltpu.roll(slot_tenant, (nd - k) * CAP, 1)
        tens_ref[k] = jnp.where(mine, turned, 0.0)
    for k in range(1, nd):
        send(tens_ref.at[k], tenr.at[d], tsend.at[k], trecv.at[k], {"dp": ds_[k]})

    def dispatch(which, j):
        s = near[j]
        own, gathered, sel, buf = (
            (tok_ref, tokg, selx, xbuf) if which == 0 else (cot_ref, cotg, seld, dbuf)
        )
        if j:
            remote(
                own, gathered.at[s], zsend.at[which, s, 0], zrecv.at[which, s], {"expert": zs[1]}
            ).wait_recv()
            line_send(gathered.at[s], gathered.at[s], which, s, 0, (s > z) & (z > 0))
            line_send(gathered.at[s], gathered.at[s], which, s, 1, (s < z) & (z < nz - 1))
            if which == 0 and j == nz - 2:
                own_line(1)
            block = gathered[s]
        else:
            block = own[...]
        for k in list(range(1, nd)) + [0]:
            e = ds_[k]
            picked = mm(pick_ref[e], block)
            if which:
                picked = picked * slotw_ref[e, :, 0:1]
            picked = picked.astype(jnp.bfloat16)
            if k:
                sel[j, e] = picked
                send(
                    sel.at[j, e],
                    buf.at[s, d],
                    dsend.at[which, j, k],
                    drecv.at[which, j, k],
                    {"dp": e},
                )
            else:
                buf[s, d] = picked

    def arrived(which, j):
        s = near[j]
        sel, buf = (selx, xbuf) if which == 0 else (seld, dbuf)
        for k in range(1, nd):
            remote(
                sel.at[j, ds_[k]],
                buf.at[s, db[k]],
                dsend.at[which, j, k],
                drecv.at[which, j, k],
                {"dp": ds_[k]},
            ).wait_recv()
        return s

    def part_out(kind, value):
        tot = jnp.where(ten() > 0.5, value[RANK:], value[:RANK])
        part[kind, z] = tot
        for k in range(1, nz):
            send(
                part.at[kind, z],
                part.at[kind, z],
                psend.at[kind, k],
                precv.at[kind, k],
                {"expert": zs[k]},
            )

    def part_in(kind, scale):
        for k in range(1, nz):
            remote(
                part.at[kind, z],
                part.at[kind, zb[k]],
                psend.at[kind, k],
                precv.at[kind, k],
                {"expert": zs[k]},
            ).wait_recv()
        tot = part[kind, 0]
        for i in range(1, nz):
            tot = tot + part[kind, i]
        tot = tot * scale
        high = ten() > 0.5
        return jnp.concatenate([jnp.where(high, 0.0, tot), jnp.where(high, tot, 0.0)], axis=0)

    def ten():
        tot = tenr[0, 0:1]
        for i in range(1, nd):
            tot = tot + tenr[i, 0:1]
        return tot

    def tiles(body):
        def run(i, carry):
            body(pl.ds(pl.multiple_of(i * tile, tile), tile))
            return carry

        lax.fori_loop(0, ffl // tile, run, 0)

    def forward(j):
        s = arrived(0, j)
        weight(0, s).wait()
        weight(1, s).wait()

        def body(cols):
            xs = xbuf[s].reshape(rows, width)
            g = mm(xs, wg[s, :, cols])
            u = mm(xs, wu[s, :, cols])
            if j:
                gate[:, cols] += g
                up[:, cols] += u
            else:
                gate[:, cols] = g
                up[:, cols] = u

        tiles(body)

    dispatch(0, 0)
    tenr[d] = tens_ref[0]
    for k in range(1, nd):
        remote(
            tens_ref.at[k], tenr.at[db[k]], tsend.at[k], trecv.at[k], {"dp": ds_[k]}
        ).wait_recv()
    dispatch(0, 1)
    forward(0)
    part_out(0, mm_nt(aupt_ref[...], xbuf[z].reshape(rows, width)))
    for j in range(2, nz):
        dispatch(0, j)
        forward(j - 1)
    dispatch(1, 0)
    forward(nz - 1)
    low_a_t = part_in(0, 1.0)
    low_a = low_a_t.T.astype(jnp.bfloat16)
    low_a_t = low_a_t.astype(jnp.bfloat16)
    dispatch(1, 1)

    def act(cols):
        g = gate[:, cols]
        u = up[:, cols] + adapter_scale * mm(low_a, bup_ref[:, cols])
        a = g / (1.0 + jnp.exp(-g))
        gate[:, cols] = a
        hidden[:, cols] = (a * u).astype(jnp.bfloat16)

    tiles(act)
    part_out(2, mm_nt(adnt_ref[...], hidden[...]))
    dispatch(1, 2)

    def down(k, low_c):
        c = zs[k]
        weight(2, c).wait()
        for t in range(0, width, 256):
            n = min(256, width - t)
            r = mm(hidden[...], wd[c, :, t : t + n])
            if k == 0:
                r = r + adapter_scale * mm(low_c, bdn_ref[:, t : t + n])
            outs[c, :, :, t : t + n] = r.astype(jnp.bfloat16).reshape(nd, CAP, n)
        for i in range(1, nd):
            send(
                outs.at[c, ds_[i]], back.at[c, d], osend.at[k, i], orecv.at[k, i], {"dp": ds_[i]}
            )
        back[c, d] = outs[c, d]

    def combine(k):
        c = zs[k]
        for i in range(1, nd):
            remote(
                outs.at[c, ds_[i]], back.at[c, db[i]], osend.at[k, i], orecv.at[k, i], {"dp": ds_[i]}
            ).wait_recv()
        b = back[c].reshape(rows, width)
        m = mm(c0_ref[...], b) * rwc_ref[0, :, 0:1] + mm(c1_ref[...], b) * rwc_ref[1, :, 0:1]
        if k:
            mixs[c] = m.astype(jnp.bfloat16)
            send(mixs.at[c], mixr.at[z], msend.at[k], mrecv.at[k], {"expert": c})
        else:
            mixo[...] = m

    def backward(j, low_d):
        s = arrived(1, j) if j else z

        def body(cols):
            r = mm_nt(dbuf[s].reshape(rows, width), wd[s, cols, :])
            if j == 0:
                up[:, cols] = r
            elif j < nz - 1:
                up[:, cols] += r
            else:
                r = r + up[:, cols] + mm(low_d, adnt_ref[:, cols])
                dhid[:, cols] = (r * gate[:, cols]).astype(jnp.bfloat16)

        tiles(body)

    down(1, None)
    for j in range(3, nz):
        dispatch(1, j)
    for k in range(2, nz):
        down(k, None)
    low_c_t = part_in(2, 1.0)
    low_c = low_c_t.T.astype(jnp.bfloat16)
    down(0, low_c)
    arrived(1, 0)
    part_out(1, mm_nt(bdn_ref[...], dbuf[z].reshape(rows, width)))
    low_c_t = low_c_t.astype(jnp.bfloat16)
    combine(1)
    gbd_ref[...] = adapter_scale * mm(low_c_t, dbuf[z].reshape(rows, width))
    return_steps = list(range(2, nz)) + [0]
    low_d = None
    for j in range(nz):
        if j == nz - 1:
            low_d_t = part_in(1, adapter_scale)
            low_d = low_d_t.T.astype(jnp.bfloat16)
            low_d_t = low_d_t.astype(jnp.bfloat16)
        backward(j, low_d)
        if j < len(return_steps):
            combine(return_steps[j])
    part_out(3, mm_nt(bup_ref[...], dhid[...]))

    def grads(cols):
        gadt_ref[:, cols] = mm(low_d_t, hidden[:, cols])
        gbu_ref[:, cols] = adapter_scale * mm(low_a_t, dhid[:, cols])

    tiles(grads)
    low_z = part_in(3, adapter_scale)
    hi = low_z.astype(jnp.bfloat16)
    lo = (low_z - hi.astype(jnp.float32)).astype(jnp.bfloat16)
    xs = xbuf[z].reshape(rows, width)
    gaut_ref[...] = mm(hi, xs) + mm(lo, xs)
    total = mixo[...]
    for k in range(1, nz):
        remote(mixs.at[zs[k]], mixr.at[zb[k]], msend.at[k], mrecv.at[k], {"expert": zs[k]}).wait_recv()
        total = total + mixr[zb[k]].astype(jnp.float32)
    mixed_ref[...] = total.astype(jnp.bfloat16)
    for copy in pending:
        copy.wait_send()
    for copy, may in line_sends:
        pl.when(may)(copy.wait_send)


def hand_over(*refs):
    half = len(refs) // 2
    for i in range(half):
        refs[half + i][...] = refs[i][...]


def on_device_fused(
    tokens,
    cotangent,
    routes,
    route_weight,
    tenant,
    w_gate,
    w_up,
    w_down,
    a_up,
    b_up,
    a_down,
    b_down,
):
    nz, nd = lax.axis_size("expert"), lax.axis_size("dp")
    tok_count, width = tokens.shape
    ffl = w_gate.shape[2]
    rows = nd * CAP
    vmem = pl.BlockSpec(memory_space=pltpu.VMEM)
    hbm = pl.BlockSpec(memory_space=pl.ANY)
    bf, f32 = jnp.bfloat16, jnp.float32
    dma = pltpu.SemaphoreType.DMA
    wide = TENANTS * RANK
    results = pl.pallas_call(
        functools.partial(fused_kernel, nz, nd),
        out_shape=(
            jax.ShapeDtypeStruct((tok_count, width), bf),
            jax.ShapeDtypeStruct((wide, width), f32),
            jax.ShapeDtypeStruct((wide, ffl), f32),
            jax.ShapeDtypeStruct((wide, ffl), f32),
            jax.ShapeDtypeStruct((wide, width), f32),
        ),
        in_specs=[vmem] * 5 + [hbm] * 3 + [vmem] * 4,
        out_specs=[vmem] * 5,
        scratch_shapes=[
            pltpu.VMEM((nd, CAP, tok_count), bf),
            pltpu.VMEM((nd, CAP, tok_count), f32),
            pltpu.VMEM((nd, 8, rows), f32),
            pltpu.VMEM((tok_count, rows), bf),
            pltpu.VMEM((tok_count, rows), bf),
            pltpu.VMEM((TOP, tok_count, tok_count), f32),
            pltpu.VMEM((nz, width, ffl), bf),
            pltpu.VMEM((nz, width, ffl), bf),
            pltpu.VMEM((nz, ffl, width), bf),
            pltpu.VMEM((nz, tok_count, width), bf),
            pltpu.VMEM((nz, tok_count, width), bf),
            pltpu.VMEM((nz, nd, CAP, width), bf),
            pltpu.VMEM((nz, nd, CAP, width), bf),
            pltpu.VMEM((nz, nd, CAP, width), bf),
            pltpu.VMEM((nz, nd, CAP, width), bf),
            pltpu.VMEM((rows, ffl), f32),
            pltpu.VMEM((rows, ffl), f32),
            pltpu.VMEM((rows, ffl), bf),
            pltpu.VMEM((rows, ffl), bf),
            pltpu.VMEM((nz, nd, CAP, width), bf),
            pltpu.VMEM((nz, nd, CAP, width), bf),
            pltpu.VMEM((nz, tok_count, width), bf),
            pltpu.VMEM((nz, tok_count, width), bf),
            pltpu.VMEM((tok_count, width), f32),
            pltpu.VMEM((nd, 8, rows), f32),
            pltpu.VMEM((4, nz, RANK, rows), f32),
            dma((3, nz)),
            dma((2, nz, 2)),
            dma((2, nz)),
            dma((2, nz, nd)),
            dma((2, nz, nd)),
            dma((nd,)),
            dma((nd,)),
            dma((4, nz)),
            dma((4, nz)),
            dma((nz, nd)),
            dma((nz, nd)),
            dma((nz,)),
            dma((nz,)),
        ],
        compiler_params=pltpu.CompilerParams(
            collective_id=0, has_side_effects=True, vmem_limit_bytes=62 * 1024 * 1024
        ),
    )(
        tokens,
        cotangent,
        routes.T,
        route_weight.T,
        tenant[None],
        w_gate,
        w_up,
        w_down,
        a_up[0].T,
        b_up[0],
        a_down[0].T,
        b_down[0],
    )
    count = len(results)
    mixed, gaut, gbu, gadt, gbd = pl.pallas_call(
        hand_over,
        out_shape=tuple(jax.ShapeDtypeStruct(r.shape, r.dtype) for r in results),
        in_specs=[vmem] * count,
        out_specs=[vmem] * count,
    )(*results)
    return mixed, gaut.T[None], gbu[None], gadt.T[None], gbd[None]


def on_device(*args):
    nz, nd = lax.axis_size("expert"), lax.axis_size("dp")
    tok_count, width = args[0].shape
    ffl = args[5].shape[2]
    weight_bytes = 6 * nz * width * ffl
    row_bytes = 12 * nz * nd * CAP * width
    fits = weight_bytes + row_bytes <= 50 * 1024 * 1024
    if width % 128 or ffl % 256 or tok_count % 128 or (nd * CAP) % 128 or not fits:
        return on_device_plain(*args)
    return on_device_fused(*args)


def solution(mesh):
    return jax.shard_map(
        on_device,
        mesh=mesh,
        in_specs=(
            P(("groups", "dp"), "expert"),
            P(("groups", "dp"), "expert"),
            P(("groups", "dp"), None),
            P(("groups", "dp"), None),
            P(("groups", "dp")),
            P("dp", None, "expert"),
            P("dp", None, "expert"),
            P("dp", "expert", None),
            P("dp", "expert", None),
            P("dp", None, "expert"),
            P("dp", "expert", None),
            P("dp", None, "expert"),
        ),
        out_specs=(
            P(("groups", "dp"), "expert"),
            P(("groups", "dp"), "expert", None),
            P(("groups", "dp"), None, "expert"),
            P(("groups", "dp"), "expert", None),
            P(("groups", "dp"), None, "expert"),
        ),
        check_vma=False,
    )
```
